256 devices in a mesh: dp: 64 (over z, x, y_hi), mp: 4 (over y_lo, core).
Axes of the slice: x: 4, y: 4 (y_hi: 2, y_lo: 2; y = y_hi * 2 + y_lo), z: 8, core: 2. Of those that a mesh axis runs over, the one named last changes fastest.
Arguments:
- query_in: bfloat16 [65536, 3072], P('dp', 'mp'), may hold values from -72 to 72
- key_in: bfloat16 [65536, 3072], P('dp', 'mp'), may hold values from -72 to 72
- value_in: bfloat16 [65536, 3072], P('dp', 'mp'), may hold values from -16 to 16
- grad_out: bfloat16 [65536, 3072], P('dp', 'mp'), may hold values from -100 to 100
- out_weight: bfloat16 [3072, 3072], P('dp', 'mp'), may hold values from -0.109375 to 0.109375
- query_gain: float32 [24, 128], P('mp'), may hold values from 0.5 to 5.2
- key_gain: float32 [24, 128], P('mp'), may hold values from 0.5 to 5.2
Outputs:
- grad_query: bfloat16 [65536, 3072], P('dp', 'mp')
- grad_key: bfloat16 [65536, 3072], P('dp', 'mp')
- grad_value: bfloat16 [65536, 3072], P('dp', 'mp')
- grad_weight: float32 [3072, 3072], P('dp', 'mp')
- grad_query_gain: float32 [24, 128], P('mp')
- grad_key_gain: float32 [24, 128], P('mp')
The draws below stay inside these ranges and needn't reach their ends.
All inputs are finite; a program needn't handle non-finite values.
Results may differ from the reference program's by a relative error of at most 0.02.
The reference program's roundings to bfloat16 on the way (of `query_hat`, `probs_low`, `attended`, `grad_attended` and `grad_scores`) count: a program that leaves them out, or rounds other values in their place, can miss the bound.
Values may be sent and summed in bfloat16 or wider, within the bound.
A program may use at most 128 MiB of HBM per device.

```python
import math
import jax
import jax.numpy as jnp
from jax import lax

D = 3072
HEADS = 24
HD = 128
PATCH = 256
HW = 3072
TOKENS = 65536


def token_scales(key):
    rows = jax.random.uniform(jax.random.fold_in(key, 71), (TOKENS, 1), jnp.float32, 0.0, math.log(4.0))
    cols = jax.random.uniform(jax.random.fold_in(key, 72), (1, HW), jnp.float32, math.log(0.5), math.log(4.0))
    return (jnp.exp(rows), jnp.exp(cols))


def drawn_heads(key):
    flags = jax.random.bernoulli(jax.random.fold_in(key, 73), 0.5, (HEADS,))
    chosen = jax.random.randint(jax.random.fold_in(key, 74), (), 0, HEADS)
    flags = jnp.logical_or(flags, jnp.arange(HEADS) == chosen)
    return flags.astype(jnp.float32)


def query_values(key, tied):
    rows, cols = token_scales(key)
    gauss = jnp.clip(jax.random.normal(jax.random.fold_in(key, 81), (TOKENS, HW), jnp.float32), -4.0, 4.0)
    raw = gauss
    flags = jnp.repeat(drawn_heads(key), HD)[None, :]
    odd = (jnp.arange(TOKENS) % 2 == 1).astype(jnp.float32)[:, None]
    mix = tied * odd * flags
    raw = raw * (1.0 - mix)
    return raw * rows * cols


def gain_values(key, salt, lower, upper, tied):
    flags = drawn_heads(key).reshape(HEADS, 1)
    base = jnp.exp(jax.random.uniform(jax.random.fold_in(key, salt), (HEADS, HD), jnp.float32, math.log(lower), math.log(upper)))
    return base * (1.0 - tied * flags)


def draw_query_in(key, part):
    values = query_values(key, 0.0)
    return values.astype(jnp.bfloat16)


def draw_key_in(key, part):
    rows, cols = token_scales(key)
    key = jax.random.fold_in(key, 5)
    values = jnp.clip(jax.random.normal(key, (TOKENS, HW), jnp.float32), -4.0, 4.0) * rows * cols
    return values.astype(jnp.bfloat16)


def draw_query_gain(key, part):
    values = gain_values(key, 91, 0.5, 2.0, 0.0)
    return values.astype(jnp.float32)


def draw_key_gain(key, part):
    values = gain_values(key, 95, 0.5, 2.0, 0.0)
    return values.astype(jnp.float32)


def draw_grad_out(key, part):
    key = jax.random.fold_in(key, 7)
    second = jax.random.fold_in(key, 1)
    third = jax.random.fold_in(key, 2)
    fourth = jax.random.fold_in(key, 3)
    position = jnp.arange(TOKENS, dtype=jnp.float32) / TOKENS
    rising = (1.0 + 2.0 * position)[:, None]
    base = jnp.clip(jax.random.normal(second, (TOKENS, D), jnp.float32), -4.0, 4.0)
    rows = jnp.exp(jax.random.uniform(third, (TOKENS, 1), jnp.float32, math.log(0.5), math.log(2.0)))
    cols = jnp.exp(jax.random.uniform(fourth, (1, D), jnp.float32, math.log(0.5), math.log(2.0)))
    return (base * rising * rows * cols).astype(jnp.bfloat16)


def strengthened(entries, rng, source, target, parts, factor):
    owner, partner = [(jnp.arange(entries.shape[dim]) // (entries.shape[dim] // parts)).reshape([-1 if axis == dim else 1 for axis in range(entries.ndim)]) for dim in (source, target)]
    chosen = jax.random.permutation(rng, parts)[partner]
    strong = (owner == chosen) | (owner == (partner + parts // 2) % parts)
    return jnp.where(strong, factor * entries, entries)


def levels(key, shape, cuts, low, largest):
    level, own = 1.0, jax.random.fold_in(key, 6)
    for axis_at, shards_of in cuts:
        draws = jnp.exp(jax.random.uniform(jax.random.fold_in(own, axis_at), (shards_of,), jnp.float32, low / len(cuts), largest / len(cuts)))
        level = level * jnp.repeat(draws, shape[axis_at] // shards_of).reshape([-1 if axis == axis_at else 1 for axis in range(len(shape))])
    return level


def gaussian(own_key, shape, deviation, most, cuts=(), held_as=jnp.bfloat16):
    result = jax.random.normal(own_key, shape, jnp.float32) * deviation
    if len(cuts) > 0:
        result = levels(own_key, shape, cuts, -0.22, 0.18) * result
    return jnp.clip(result, min=-most, max=most).astype(held_as)


def noise_with(own_key, dims, scale, most, pieces, heavy, kind=jnp.bfloat16):
    array = scale * jax.random.normal(own_key, dims, jnp.float32)
    if pieces:
        array = array * levels(own_key, dims, pieces, -0.22, 0.18)
    return jnp.clip(strengthened(array, jax.random.fold_in(own_key, 3), *heavy), -most, most).astype(kind)


def setup_inputs(seed: int = 0) -> dict:
    splits = jax.random.split(jax.random.key(seed), 8)
    return {
        "query_in": draw_query_in(jax.random.fold_in(splits[7], 71), 0),
        "key_in": draw_key_in(jax.random.fold_in(splits[7], 71), 0),
        "value_in": noise_with(splits[2], (TOKENS, HW), 1.0, 16.0, ((0, 64), (1, 4)), (0, 1, 64, 4.0)),
        "grad_out": draw_grad_out(jax.random.fold_in(splits[7], 71), 0),
        "out_weight": gaussian(splits[4], (HW, D), HW ** -0.5, 0.109375, ((0, 64), (1, 4))),
        "query_gain": draw_query_gain(jax.random.fold_in(splits[7], 71), 0),
        "key_gain": draw_key_gain(jax.random.fold_in(splits[7], 71), 0),
    }


epsilon = 1e-06

def head_norm(values):
    centred = values - lax.optimization_barrier(jnp.mean(values, axis=-1, keepdims=True))
    inverse = lax.rsqrt(lax.optimization_barrier(jnp.mean(centred * centred, axis=-1, keepdims=True)) + epsilon)
    return (centred * inverse, inverse)

def norm_back(grad_hat, normed, inverse, gain):
    upper = grad_hat * gain
    spread = lax.optimization_barrier(jnp.mean(upper * normed, axis=-1, keepdims=True))
    return (upper - lax.optimization_barrier(jnp.mean(upper, axis=-1, keepdims=True)) - normed * spread) * inverse

def reference(query_in, key_in, value_in, grad_out, out_weight, query_gain, key_gain):
    factor = 1.0 / math.sqrt(HD)
    images = TOKENS // PATCH
    layout = (PATCH, HEADS, HD)

    def per_image(carry, index):
        weight_sum, query_sum, key_sum = carry
        start = index.astype(jnp.int32) * PATCH
        query_rows = lax.dynamic_slice_in_dim(query_in, start, PATCH, 0).astype(jnp.float32).reshape(layout)
        key_rows = lax.dynamic_slice_in_dim(key_in, start, PATCH, 0).astype(jnp.float32).reshape(layout)
        value_rows = lax.dynamic_slice_in_dim(value_in, start, PATCH, 0).reshape(layout).astype(jnp.float32)
        grad_rows = lax.dynamic_slice_in_dim(grad_out, start, PATCH, 0)
        query_norm, query_inverse = head_norm(query_rows)
        key_norm, key_inverse = head_norm(key_rows)
        query_hat = (query_norm * query_gain).astype(jnp.bfloat16).astype(jnp.float32)
        key_hat = (key_norm * key_gain).astype(jnp.bfloat16).astype(jnp.float32)
        scores = jnp.einsum('qhd,khd->hqk', query_hat, key_hat) * factor
        top = lax.optimization_barrier(jnp.max(scores, axis=-1, keepdims=True))
        expo = jnp.exp(scores - top)
        probs = expo / lax.optimization_barrier(jnp.sum(expo, axis=-1, keepdims=True))
        probs_low = probs.astype(jnp.bfloat16).astype(jnp.float32)
        attended = jnp.einsum('hqk,khd->qhd', probs_low, value_rows).astype(jnp.bfloat16).reshape(PATCH, HW)
        grad_attended = jnp.dot(grad_rows, out_weight.T, preferred_element_type=jnp.float32).astype(jnp.bfloat16)
        weight_sum = weight_sum + jnp.dot(attended.T, grad_rows, preferred_element_type=jnp.float32)
        grad_heads = grad_attended.astype(jnp.float32).reshape(layout)
        grad_value = jnp.einsum('hqk,qhd->khd', probs_low, grad_heads).astype(jnp.bfloat16)
        grad_probs = jnp.einsum('qhd,khd->hqk', grad_heads, value_rows)
        inner = lax.optimization_barrier(jnp.sum(probs * grad_probs, axis=-1, keepdims=True))
        grad_scores = (probs * (grad_probs - inner) * factor).astype(jnp.bfloat16).astype(jnp.float32)
        grad_qhat = jnp.einsum('hqk,khd->qhd', grad_scores, key_hat)
        grad_khat = jnp.einsum('hqk,qhd->khd', grad_scores, query_hat)
        query_sum = query_sum + lax.optimization_barrier(jnp.sum(grad_qhat * query_norm, axis=0))
        key_sum = key_sum + lax.optimization_barrier(jnp.sum(grad_khat * key_norm, axis=0))
        grad_query = norm_back(grad_qhat, query_norm, query_inverse, query_gain).astype(jnp.bfloat16)
        grad_key = norm_back(grad_khat, key_norm, key_inverse, key_gain).astype(jnp.bfloat16)
        outputs = (grad_query.reshape(PATCH, HW), grad_key.reshape(PATCH, HW), grad_value.reshape(PATCH, HW))
        return ((weight_sum, query_sum, key_sum), outputs)
    start_carry = (jnp.zeros((HW, D), jnp.float32), jnp.zeros((HEADS, HD), jnp.float32), jnp.zeros((HEADS, HD), jnp.float32))
    carry, stacked = lax.scan(per_image, start_carry, jnp.arange(images, dtype=jnp.int32))
    grad_query = stacked[0].reshape(TOKENS, HW)
    grad_key = stacked[1].reshape(TOKENS, HW)
    grad_value = stacked[2].reshape(TOKENS, HW)
    return (grad_query, grad_key, grad_value, carry[0], carry[1], carry[2])
```

```python
import math

import jax
import jax.numpy as jnp
from jax import lax
from jax.experimental import pallas as pl
from jax.experimental.pallas import tpu as pltpu
from jax.sharding import PartitionSpec as P

PATCH = 256
HD = 128
EPS = 1e-06
F32 = jnp.float32
BF16 = jnp.bfloat16
MESH = pl.DeviceIdType.MESH
NZ, NX = 8, 4
FACTOR = 1.0 / math.sqrt(HD)

NN = (((1,), (0,)), ((), ()))
NT = (((1,), (1,)), ((), ()))
TN = (((0,), (0,)), ((), ()))


def dot(a, b, dims):
    return lax.dot_general(a, b, dims, preferred_element_type=F32)


def device(z, x, yh, yl, c):
    return {"dp": (z * NX + x) * 2 + yh, "mp": yl * 2 + c}


def kernel(
    q_hbm, k_hbm, v_hbm, g_hbm, w_hbm, qgain, kgain,
    gq_hbm, gk_hbm, gv_hbm, gw_out, qg_out, kg_out,
    qb, kb, vb, G, W7, P7, attT, qh, kh, qn, kn, probs, gatt,
    raz, rax, rbx, rbz, fin, gacc, gbuf,
    ld_sem, own_sem, out_sem,
    wr_s, wr_r, gy_s, gy_r, gc_s, gc_r, gf_s, gf_r,
    ag_s, ag_r, rs_s, rs_r, fin_s, fin_r, ga_s, ga_r,
):
    dp, mp = lax.axis_index("dp"), lax.axis_index("mp")
    z, x, yh = dp // 8, (dp // 2) % 4, dp % 2
    yl, c = mp // 2, mp % 2
    zl, yb, cb = z // 4, (z // 2) % 2, z % 2
    m_src, zl_src = z // 2, z % 2

    def to_plane(half):
        return zl_src * 4 + yh * 2 + c, x, half, m_src // 2, m_src % 2

    def to_owner(s):
        return mp * 2 + zl, x, yb, s, cb

    def is_me(d):
        same = (d[0] == z) & (d[1] == x) & (d[2] == yh)
        return same & (d[3] == yl) & (d[4] == c)

    rem = lax.rem

    barrier = pltpu.get_barrier_semaphore()

    def greet(d):
        pl.semaphore_signal(barrier, inc=1, device_id=device(*d), device_id_type=MESH)

    j = x * 2 + yh
    for step in range(1, 8):
        greet((rem(z + step, 8), x, yh, yl, c))
        jj = rem(j + step, 8)
        greet((z, jj // 2, jj % 2, yl, c))
    greet((z, x, yh, 1 - yl, c))
    greet((z, x, yh, yl, 1 - c))
    count = jnp.int32(20)
    for d in (to_plane(0), to_plane(1), to_owner(0), to_owner(1)):
        mine = is_me(d)
        count = count - mine.astype(jnp.int32)
        pl.when(jnp.logical_not(mine))(lambda d=d: greet(d))

    def load(a, i):
        src, dst = ((q_hbm, qb), (k_hbm, kb), (v_hbm, vb))[a]
        rows = pl.ds(i * PATCH, PATCH)
        return pltpu.make_async_copy(src.at[rows], dst.at[rows], ld_sem.at[a, i])

    for i in range(4):
        for a in range(3):
            load(a, i).start()
    own_load = pltpu.make_async_copy(g_hbm, G.at[mp], own_sem)
    own_load.start()
    pl.semaphore_wait(barrier, count)

    def remote(src, dst, send, recv, d):
        return pltpu.make_async_remote_copy(
            src_ref=src, dst_ref=dst, send_sem=send, recv_sem=recv,
            device_id=device(*d), device_id_type=MESH,
        )

    def w_copy(half):
        return remote(w_hbm, W7.at[yl, c, zl_src, x, yh], wr_s.at[half], wr_r.at[yl], to_plane(half))

    for half in range(2):
        mine = is_me(to_plane(half))
        pl.when(jnp.logical_not(mine))(lambda half=half: w_copy(half).start())
        pl.when(mine)(
            lambda: pltpu.make_async_copy(
                w_hbm, W7.at[yl, c, zl_src, x, yh], wr_r.at[yl]
            ).start()
        )

    def w_arrive(s):
        here = W7.at[s, cb, zl, x, yb]
        pltpu.make_async_copy(here, here, wr_r.at[s]).wait()

    def g_rows(ref, i):
        return ref.at[pl.ds(i * PATCH, PATCH)]

    def gy(i, block):
        return remote(g_rows(g_hbm, i), g_rows(G.at[block], i), gy_s.at[i], gy_r.at[i], (z, x, yh, 1 - yl, c))

    def gc(i, block):
        return remote(g_rows(g_hbm, i), g_rows(G.at[block], i), gc_s.at[i], gc_r.at[i], (z, x, yh, yl, 1 - c))

    def gf(i, block):
        part = g_rows(G.at[block], i)
        return remote(part, part, gf_s.at[i], gf_r.at[i], (z, x, yh, yl, 1 - c))

    near = (1 - yl) * 2 + c
    core = yl * 2 + 1 - c
    far = (1 - yl) * 2 + 1 - c
    for i in range(4):
        gy(i, mp).start()
    for i in range(4):
        gc(i, mp).start()

    def g_forward(i):
        gy(i, near).wait_recv()
        gf(i, near).start()

    def half_of(ref, which):
        lead = (slice(None),) * (len(ref.shape) - 1)
        return ref.at[lead + (pl.ds(which * 384, 384),)]

    def side(st):
        return yl if st == 0 else 1 - yl

    def view(ref, st, axis, wide, idx):
        s = side(st)
        if axis == "z":
            a, b, d = idx // 4, (idx // 2) % 2, idx % 2
            return ref.at[s, d, a, :, b] if wide else ref.at[s, d, a, x, b]
        return ref.at[s, :, :, idx, :] if wide else ref.at[s, cb, zl, idx, yb]

    def ring(axis):
        return (NZ, z) if axis == "z" else (NX, x)

    def neighbour(axis, way):
        if axis == "z":
            return rem(z + way + NZ, NZ), x, yh, yl, c
        return z, rem(x + way + NX, NX), yh, yl, c

    AG = ((("x", False), ("z", True)), (("z", False), ("x", True)))

    def ag_part(st, ph, way, step, back):
        axis, wide = AG[st][ph]
        n, me = ring(axis)
        ref = view(W7, st, axis, wide, rem(me - way * back + 2 * n, n))
        return half_of(ref, 0 if way > 0 else 1) if step == n // 2 - 1 else ref

    def ag_copy(st, ph, way, step, back):
        ref = ag_part(st, ph, way, step, back)
        k = 0 if way > 0 else 1
        return remote(
            ref, ref, ag_s.at[st, ph, k, step], ag_r.at[st, ph, k, step], neighbour(AG[st][ph][0], way)
        )

    def ag_send(st, ph, step):
        for way in (1, -1):
            ag_copy(st, ph, way, step, step).start()

    def ag_event(st, ph, step):
        steps = ring(AG[st][ph][0])[0] // 2
        for way in (1, -1):
            ag_copy(st, ph, way, step, step + 1).wait_recv()
            if step + 1 < steps:
                ag_copy(st, ph, way, step + 1, step + 1).start()
        if step + 1 == steps and ph == 0:
            ag_send(st, 1, 0)

    RS = ((("z", True), ("x", False)), (("x", True), ("z", False)))
    landing = ((raz, rax), (rbx, rbz))

    def rs_copy(st, ph, way, step, off):
        axis, wide = RS[st][ph]
        n, me = ring(axis)
        k = 0 if way > 0 else 1
        ref = view(P7, st, axis, wide, rem(me + way * off + 2 * n, n))
        dst = landing[st][ph].at[k, step]
        if step == 0:
            ref, dst = half_of(ref, k), half_of(dst, k)
        return remote(ref, dst, rs_s.at[st, ph, k, step], rs_r.at[st, ph, k, step], neighbour(axis, way))

    def rs_send(st, ph, step):
        axis = RS[st][ph][0]
        for way in (1, -1):
            rs_copy(st, ph, way, step, ring(axis)[0] // 2 - step).start()

    def rs_add(st, ph, way, step, off):
        axis, wide = RS[st][ph]
        n, me = ring(axis)
        k = 0 if way > 0 else 1
        ref = view(P7, st, axis, wide, rem(me + way * off + 2 * n, n))
        got = landing[st][ph].at[k, step]
        if step == 0:
            ref, got = half_of(ref, k), half_of(got, k)

        def add(a, b):
            a[...] = (a[...].astype(F32) + b[...].astype(F32)).astype(BF16)

        if not wide:
            add(ref, got)
        elif axis == "z":
            def body(t, carry):
                add(ref.at[t], got.at[t])
                return carry
            lax.fori_loop(0, NX, body, 0)
        else:
            def body(t, carry):
                add(ref.at[t // 4, (t // 2) % 2, t % 2], got.at[t // 4, (t // 2) % 2, t % 2])
                return carry
            lax.fori_loop(0, NZ, body, 0)

    def fin_copy(st):
        s = side(st)
        return remote(P7.at[s, cb, zl, x, yb], fin.at[yh], fin_s.at[st], fin_r.at[yh], to_owner(s))

    def rs_event(st, ph, step):
        axis = RS[st][ph][0]
        steps = ring(axis)[0] // 2
        for way in (1, -1):
            rs_copy(st, ph, way, step, steps - 1 - step).wait_recv()
            rs_add(st, ph, way, step, steps - 1 - step)
            if step + 1 < steps:
                rs_copy(st, ph, way, step + 1, steps - 1 - step).start()
        if step + 1 == steps:
            if ph == 0:
                rs_send(st, 1, 0)
            else:
                s = side(st)
                mine = is_me(to_owner(s))
                pl.when(jnp.logical_not(mine))(lambda: fin_copy(st).start())
                pl.when(mine)(
                    lambda: pltpu.make_async_copy(
                        P7.at[s, cb, zl, x, yb], fin.at[yh], fin_r.at[yh]
                    ).start()
                )

    def normed(ref, gains, h, rows, cols):
        v = ref[rows, cols].astype(F32)
        v = v - jnp.mean(v, axis=-1, keepdims=True)
        inverse = lax.rsqrt(jnp.mean(v * v, axis=-1, keepdims=True) + EPS)
        return v * inverse, inverse

    def place(it):
        i, h = it // 6, it % 6
        rows = pl.ds(pl.multiple_of(i * PATCH, PATCH), PATCH)
        cols = pl.ds(pl.multiple_of(h * HD, HD), HD)
        return i, h, rows, cols

    def forward(it):
        i, h, rows, cols = place(it)
        a, _ = normed(qb, qgain, h, rows, cols)
        b, _ = normed(kb, kgain, h, rows, cols)
        a_hat = (a * qgain[pl.ds(h, 1), :]).astype(BF16)
        b_hat = (b * kgain[pl.ds(h, 1), :]).astype(BF16)
        qh[rows, cols] = a_hat
        kh[rows, cols] = b_hat
        scores = dot(b_hat, a_hat, NT) * FACTOR
        expo = jnp.exp(scores - jnp.max(scores, axis=0, keepdims=True))
        p = expo * (1.0 / jnp.sum(expo, axis=0, keepdims=True))
        probs[it] = p
        att = dot(vb[rows, cols], p.astype(BF16), TN)
        attT[cols, rows] = att.astype(BF16)

    def back(grad, normal, inverse, gain):
        u = grad * gain
        spread = jnp.mean(u * normal, axis=-1, keepdims=True)
        return (u - jnp.mean(u, axis=-1, keepdims=True) - normal * spread) * inverse

    def backward(it):
        i, h, rows, cols = place(it)
        ga = gatt[rows, cols]
        p = probs[it]
        vals = vb[rows, cols]
        gp = dot(vals, ga, NT)
        inner = jnp.sum(p * gp, axis=0, keepdims=True)
        gs = (p * (gp - inner) * FACTOR).astype(BF16)
        vb[rows, cols] = dot(p.astype(BF16), ga, NN).astype(BF16)
        gk = dot(gs, qh[rows, cols], NN)
        gq = dot(gs, kh[rows, cols], TN)
        a, a_inv = normed(qb, qgain, h, rows, cols)
        b, b_inv = normed(kb, kgain, h, rows, cols)
        gacc[0, pl.ds(h, 1), :] += jnp.sum(gq * a, axis=0, keepdims=True)
        gacc[0, pl.ds(8 + h, 1), :] += jnp.sum(gk * b, axis=0, keepdims=True)
        qb[rows, cols] = back(gq, a, a_inv, qgain[pl.ds(h, 1), :]).astype(BF16)
        kb[rows, cols] = back(gk, b, b_inv, kgain[pl.ds(h, 1), :]).astype(BF16)

    def weight_partial(block):
        s, d = block // 2, block % 2

        def body(t, carry):
            rows = pl.ds(pl.multiple_of(t * 384, 128), 384)
            part = dot(attT[rows, :], G[block], NN).astype(BF16)
            P7[s, d, t] = part.reshape(4, 2, 48, 768)
            return carry

        lax.fori_loop(0, 2, body, 0)

    def attended_grad(t):
        rows = pl.ds(pl.multiple_of(t * 512, 512), 512)
        total = None
        for block in range(4):
            w = W7[block // 2, block % 2].reshape(768, 768)
            part = dot(G[block, rows, :], w, NT)
            total = part if total is None else total + part
        gatt[rows, :] = total.astype(BF16)

    def store(a, i):
        src, dst = ((qb, gq_hbm), (kb, gk_hbm), (vb, gv_hbm))[a]
        rows = pl.ds(i * PATCH, PATCH)
        return pltpu.make_async_copy(src.at[rows], dst.at[rows], out_sem.at[a, i])

    def start_gather():
        for s in range(2):
            w_arrive(s)
        ag_send(0, 0, 0)
        ag_send(1, 0, 0)

    first = {
        1: [start_gather],
        4: [lambda: ag_event(0, 0, 0), lambda: ag_event(1, 0, 0)],
        8: [lambda: ag_event(0, 0, 1), lambda: ag_event(1, 0, 1)],
        12: [lambda: g_forward(0)],
        14: [lambda: ag_event(1, 0, 2)],
        18: [lambda: ag_event(1, 0, 3)],
    }

    def first_body(it, carry):
        for i in range(4):
            @pl.when(it == i * 6)
            def _():
                for a in range(3):
                    load(a, i).wait()
        forward(it)
        for at, events in first.items():
            @pl.when(it == at)
            def _():
                for event in events:
                    event()
        return carry

    lax.fori_loop(0, 24, first_body, 0)
    own_load.wait()
    weight_partial(mp)
    ag_event(0, 1, 0)
    g_forward(1)
    for i in range(4):
        gc(i, core).wait_recv()
    weight_partial(core)
    ag_event(0, 1, 1)
    g_forward(2)
    ag_event(1, 1, 0)
    ag_event(0, 1, 2)
    rs_send(0, 0, 0)
    ag_event(1, 1, 1)
    g_forward(3)
    rs_event(0, 0, 0)
    weight_partial(near)
    for i in range(4):
        gf(i, far).wait_recv()
    weight_partial(far)
    rs_send(1, 0, 0)
    ag_event(0, 1, 3)
    gacc[...] = jnp.zeros_like(gacc)

    second = {
        2: [lambda: rs_event(0, 0, 1)],
        6: [lambda: rs_event(1, 0, 0)],
        10: [lambda: rs_event(0, 0, 2)],
        16: [lambda: rs_event(0, 0, 3)],
        19: [lambda: rs_event(0, 1, 0)],
        22: [lambda: rs_event(0, 1, 1)],
    }

    def second_body(it, carry):
        for t in range(2):
            pl.when(it == t * 12)(lambda t=t: attended_grad(t))
        backward(it)
        for i in range(4):
            @pl.when(it == i * 6 + 5)
            def _():
                for a in range(3):
                    store(a, i).start()
        for at, events in second.items():
            @pl.when(it == at)
            def _():
                for event in events:
                    event()
        return carry

    lax.fori_loop(0, 24, second_body, 0)

    def gain_copy(ph, step):
        if ph == 0:
            jj = rem(j + step, 8)
            d = (z, jj // 2, jj % 2, yl, c)
        else:
            d = (rem(z + step, 8), x, yh, yl, c)
        return remote(
            gacc.at[ph], gbuf.at[ph, step - 1], ga_s.at[ph, step - 1], ga_r.at[ph, step - 1], d
        )

    def gain_send(ph):
        for step in range(1, 8):
            gain_copy(ph, step).start()

    def gain_sum(ph):
        total = gacc[ph]
        for step in range(1, 8):
            gain_copy(ph, step).wait_recv()
            total = total + gbuf[ph, step - 1]
        return total

    gain_send(0)
    rs_event(1, 0, 1)
    gacc[1] = gain_sum(0)
    gain_send(1)
    rs_event(1, 1, 0)
    rs_event(1, 1, 1)
    gains = gain_sum(1)
    qg_out[...] = gains[0:6]
    kg_out[...] = gains[8:14]
    rs_event(1, 1, 2)
    rs_event(1, 1, 3)

    for half in range(2):
        pl.when(jnp.logical_not(is_me(to_plane(half))))(lambda half=half: w_copy(half).wait_send())
    for i in range(4):
        gy(i, mp).wait_send()
        gc(i, mp).wait_send()
        gf(i, near).wait_send()
    for st in range(2):
        for ph in range(2):
            steps = ring(AG[st][ph][0])[0] // 2
            for step in range(steps):
                for way in (1, -1):
                    ag_copy(st, ph, way, step, step).wait_send()
            steps = ring(RS[st][ph][0])[0] // 2
            for step in range(steps):
                for way in (1, -1):
                    rs_copy(st, ph, way, step, steps - step).wait_send()
    for ph in range(2):
        for step in range(1, 8):
            gain_copy(ph, step).wait_send()
    for i in range(4):
        for a in range(3):
            store(a, i).wait()
    for half in range(2):
        pltpu.make_async_copy(fin.at[half], fin.at[half], fin_r.at[half]).wait()
    for st in range(2):
        pl.when(jnp.logical_not(is_me(to_owner(side(st)))))(lambda st=st: fin_copy(st).wait_send())
    gw_out[...] = fin[0].astype(F32) + fin[1].astype(F32)


def per_device(query_in, key_in, value_in, grad_out, out_weight, query_gain, key_gain):
    vmem = pl.BlockSpec(memory_space=pltpu.VMEM)
    anywhere = pl.BlockSpec(memory_space=pl.ANY)
    tokens = jax.ShapeDtypeStruct((1024, 768), BF16)
    dma = pltpu.SemaphoreType.DMA
    act = pltpu.VMEM((1024, 768), BF16)
    big = pltpu.VMEM((2, 2, 2, 4, 2, 48, 768), BF16)
    return pl.pallas_call(
        kernel,
        out_shape=(
            tokens, tokens, tokens,
            jax.ShapeDtypeStruct((48, 768), F32),
            jax.ShapeDtypeStruct((6, 128), F32),
            jax.ShapeDtypeStruct((6, 128), F32),
        ),
        in_specs=[anywhere] * 5 + [vmem] * 2,
        out_specs=(anywhere,) * 3 + (vmem,) * 3,
        scratch_shapes=[
            act, act, act,
            pltpu.VMEM((4, 1024, 768), BF16),
            big, big,
            pltpu.VMEM((768, 1024), BF16),
            act, act,
            pltpu.VMEM((8, 128), F32), pltpu.VMEM((8, 128), F32),
            pltpu.VMEM((24, 256, 256), F32),
            act,
            pltpu.VMEM((2, 4, 4, 48, 768), BF16),
            pltpu.VMEM((2, 2, 48, 768), BF16),
            pltpu.VMEM((2, 2, 2, 2, 2, 48, 768), BF16),
            pltpu.VMEM((2, 4, 48, 768), BF16),
            pltpu.VMEM((2, 48, 768), BF16),
            pltpu.VMEM((2, 16, 128), F32),
            pltpu.VMEM((2, 7, 16, 128), F32),
            dma((3, 4)), dma, dma((3, 4)),
            dma((2,)), dma((2,)), dma((4,)), dma((4,)), dma((4,)), dma((4,)), dma((4,)), dma((4,)),
            dma((2, 2, 2, 4)), dma((2, 2, 2, 4)), dma((2, 2, 2, 4)), dma((2, 2, 2, 4)),
            dma((2,)), dma((2,)), dma((2, 7)), dma((2, 7)),
        ],
        compiler_params=pltpu.CompilerParams(
            collective_id=0, has_side_effects=True, vmem_limit_bytes=60 * 2**20
        ),
        cost_estimate=pl.CostEstimate(flops=12 * 10**9, bytes_accessed=12 * 10**6, transcendentals=1600000),
    )(query_in, key_in, value_in, grad_out, out_weight, query_gain, key_gain)


def solution(mesh):
    rows = P("dp", "mp")
    heads = P("mp", None)
    return jax.shard_map(
        per_device,
        mesh=mesh,
        in_specs=(rows, rows, rows, rows, rows, heads, heads),
        out_specs=(rows, rows, rows, rows, heads, heads),
        check_vma=False,
    )
```

```python
import heapq
import itertools
import math

import jax
import jax.numpy as jnp
from jax import lax
from jax.experimental import pallas as pl
from jax.experimental.pallas import tpu as pltpu
from jax.sharding import PartitionSpec as P

PATCH = 256
HD = 128
EPS = 1e-06
F32 = jnp.float32
BF16 = jnp.bfloat16
MESH = pl.DeviceIdType.MESH
NZ, NX = 8, 4
FACTOR = 1.0 / math.sqrt(HD)

NN = (((1,), (0,)), ((), ()))
NT = (((1,), (1,)), ((), ()))
TN = (((0,), (0,)), ((), ()))


SIDES = (1, -1)
X_OUT, X_IN = (0, 1, -1, 2), (2, 1, -1, 0)
Z_OUT, Z_IN = (0, 1, -1, 2, -2, 3, -3, 4), (4, 3, -3, 2, -2, 1, -1, 0)
GATHER = ((("x", (0,)), ("z", X_OUT)), (("z", (0,)), ("x", Z_OUT)))
REDUCE = ((("z", X_IN), ("x", (0,))), (("x", Z_IN), ("z", (0,))))
HALF = {"z": NZ // 2, "x": NX // 2}


def keys_of(kind, table):
    for st in range(2):
        for ph in range(2):
            axis, offsets = table[st][ph]
            for o in offsets:
                for way in SIDES:
                    for step in range(HALF[axis]):
                        yield (kind, st, ph, o, way, step)


SLOT = {}
for kind, table in (("ag", GATHER), ("rs", REDUCE)):
    for number, key in enumerate(keys_of(kind, table)):
        SLOT[key] = number
COPIES = len(SLOT) // 2

FULL, LATENCY = 1.6, 1.5
COST = {"fw": 0.95, "wp": 1.6, "ga": 2.7, "bw": 1.1}


def make_plan():
    now = [0.0]
    free = {}
    heap = []
    ops = []
    done = set()
    tally = itertools.count()

    def arrive(key, at):
        heapq.heappush(heap, (at, next(tally), key))

    def send(key):
        kind, st, ph, o, way, step = key
        axis = (GATHER if kind == "ag" else REDUCE)[st][ph][0]
        halved = step == (HALF[axis] - 1 if kind == "ag" else 0)
        start = max(now[0], free.get((axis, way), 0.0))
        free[axis, way] = start + (FULL / 2 if halved else FULL)
        arrive(key, free[axis, way] + LATENCY)
        ops.append(("send", key))

    def gather_ready(st, o):
        for way in SIDES:
            send(("ag", st, 1, o, way, 0))

    forwards = [sum(1 for k in keys_of("ag", GATHER) if k[5] + 1 < HALF[GATHER[k[1]][k[2]][0]])]

    def try_reduce():
        if forwards[0] or now[0] < 0:
            return
        for st, needs in ((0, ("own", "core")), (1, ("near", "far"))):
            if ("start", st) not in done and all(("wp", n) in done for n in needs):
                done.add(("start", st))
                for o in REDUCE[st][0][1]:
                    for way in SIDES:
                        send(("rs", st, 0, o, way, 0))

    def try_second(st, way, step):
        half = HALF[REDUCE[st][1][0]]
        o = way * (half - step)
        if abs(o) == half:
            o = half
        axis = REDUCE[st][0][0]
        last = HALF[axis] - 1
        ready = all(("rs", st, 0, o, w, last) in done for w in SIDES)
        if ready and (step == 0 or ("rs", st, 1, 0, way, step - 1) in done):
            key = ("rs", st, 1, 0, way, step)
            if ("sent", key) not in done:
                done.add(("sent", key))
                send(key)

    def process(key):
        ops.append(("recv", key))
        done.add(key)
        now[0] += 0.05
        if key == ("wred",):
            for st in (1, 0):
                for way in SIDES:
                    send(("ag", st, 0, 0, way, 0))
                gather_ready(st, 0)
        elif key[0] == "gy":
            arrive(("gf", key[1]), now[0] + 2.5)
        elif key == ("gain", 0):
            arrive(("gain", 1), now[0] + 3.0)
        elif key[0] == "ag":
            _, st, ph, o, way, step = key
            half = HALF[GATHER[st][ph][0]]
            if step + 1 < half:
                forwards[0] -= 1
                send(("ag", st, ph, o, way, step + 1))
            if ph == 0:
                if step + 1 < half:
                    gather_ready(st, -way * (step + 1))
                elif ("ag", st, 0, 0, -way, step) in done:
                    gather_ready(st, half)
            try_reduce()
        elif key[0] == "rs":
            _, st, ph, o, way, step = key
            half = HALF[REDUCE[st][ph][0]]
            if ph == 0:
                if step + 1 < half:
                    send(("rs", st, 0, o, way, step + 1))
                else:
                    for w in SIDES:
                        for later in range(HALF[REDUCE[st][1][0]]):
                            try_second(st, w, later)
            else:
                if step + 1 < half:
                    try_second(st, way, step + 1)
            total = [k for k in keys_of("rs", REDUCE) if k[1] == st]
            if all(k in done for k in total):
                ops.append(("final", st))

    work = [("fw", i) for i in range(12)]
    work += [("wp", n) for n in ("own", "core", "near", "far")]
    for t in range(2):
        work += [("ga", t)] + [("bw", 6 * t + i) for i in range(6)]
    gathered = set(keys_of("ag", GATHER))

    def ready(unit):
        kind, n = unit
        if kind == "wp" and n == "core":
            return ("gc",) in done
        if kind == "wp" and n == "near":
            return ("gy", 3) in done
        if kind == "wp" and n == "far":
            return ("gf", 3) in done
        if kind == "ga":
            return gathered <= done and all(("gf", i) in done for i in range(4))
        return True

    arrive(("wred",), 6.3)
    arrive(("gc",), 8.0)
    for i in range(4):
        arrive(("gy", i), 8.4 * (i + 1) + 3.5)
    while heap or work:
        if heap and heap[0][0] <= now[0]:
            process(heapq.heappop(heap)[2])
        elif work and ready(work[0]):
            unit = work.pop(0)
            ops.append(unit)
            done.add(unit)
            now[0] += COST[unit[0]]
            try_reduce()
            if unit == ("bw", 11):
                ops.append(("gain", 0))
                arrive(("gain", 0), now[0] + 3.0)
        else:
            now[0] = max(now[0], heap[0][0])
    return ops, now[0]


PLAN = make_plan()[0]
POOL = 64
SENDS = [op[1] for op in PLAN if op[0] == "send"]
ORDER = {key: n for n, key in enumerate(SENDS)}


def dot(a, b, dims):
    return lax.dot_general(a, b, dims, preferred_element_type=F32)


def device(z, x, yh, yl, c):
    return {"dp": (z * NX + x) * 2 + yh, "mp": yl * 2 + c}


def kernel(
    q_hbm, k_hbm, v_hbm, g_hbm, w_hbm, qgain, kgain,
    gq_hbm, gk_hbm, gv_hbm, gw_hbm, qg_hbm, kg_hbm,
    qb, kb, vb, G, W7, P7, attT, qh, kh, probs, gatt,
    landing, fin, gacc, gbuf, gw_out, small_sem,
    ld_sem, own_sem, out_sem,
    wr_s, wr_r, gy_s, gy_r, gc_s, gc_r, gf_s, gf_r,
    ring_s, ag_r, rs_r, fin_s, fin_r, ga_s, ga_r,
):
    dp, mp = lax.axis_index("dp"), lax.axis_index("mp")
    z, x, yh = dp // 8, (dp // 2) % 4, dp % 2
    yl, c = mp // 2, mp % 2
    m_src, zl_src = z // 2, z % 2
    rem = lax.rem

    def bits(zz):
        r = rem(zz - 2 * mp + NZ, NZ)
        upper = (r >= 1) & (r <= 4)
        t = jnp.where(upper, r - 1, rem(NZ - r, NZ))
        return upper.astype(jnp.int32), t // 2, t % 2

    z_at = {o: rem(z + o + NZ, NZ) for o in range(-4, 5)}
    x_at = {o: rem(x + o + NX, NX) for o in range(-2, 3)}
    bits_at = {o: bits(z_at[o]) for o in range(-3, 5)}
    bits_at[-4] = bits_at[4]
    zl, yb, cb = bits_at[0]

    def to_plane(half):
        target = rem(z + (2 * zl_src - 1) * (yh * 2 + c) + NZ, NZ)
        return target, x, half, m_src // 2, m_src % 2

    def to_owner(s):
        return mp * 2 + zl, x, yb, s, cb

    def is_me(d):
        same = (d[0] == z) & (d[1] == x) & (d[2] == yh)
        return same & (d[3] == yl) & (d[4] == c)

    barrier = pltpu.get_barrier_semaphore()

    def greet(d):
        pl.semaphore_signal(barrier, inc=1, device_id=device(*d), device_id_type=MESH)

    j = x * 2 + yh
    for step in range(1, 8):
        greet((rem(z + step, 8), x, yh, yl, c))
        jj = rem(j + step, 8)
        greet((z, jj // 2, jj % 2, yl, c))
    greet((z, x, yh, 1 - yl, c))
    greet((z, x, yh, yl, 1 - c))
    count = jnp.int32(20)
    for d in (to_plane(0), to_plane(1), to_owner(0), to_owner(1)):
        mine = is_me(d)
        count = count - mine.astype(jnp.int32)
        pl.when(jnp.logical_not(mine))(lambda d=d: greet(d))

    def load(a, i):
        src, dst = ((q_hbm, qb), (k_hbm, kb), (v_hbm, vb))[a]
        rows = pl.ds(i * PATCH, PATCH)
        return pltpu.make_async_copy(src.at[rows], dst.at[rows], ld_sem.at[a, i])

    for i in range(4):
        for a in range(3):
            load(a, i).start()
    own_load = pltpu.make_async_copy(g_hbm, G.at[mp], own_sem)
    own_load.start()
    pl.semaphore_wait(barrier, count)

    def remote(src, dst, send, recv, d):
        return pltpu.make_async_remote_copy(
            src_ref=src, dst_ref=dst, send_sem=send, recv_sem=recv,
            device_id=device(*d), device_id_type=MESH,
        )

    def w_copy(half):
        return remote(w_hbm, W7.at[yl, c, zl_src, x, yh], wr_s.at[half], wr_r.at[yl], to_plane(half))

    for half in range(2):
        mine = is_me(to_plane(half))
        pl.when(jnp.logical_not(mine))(lambda half=half: w_copy(half).start())
        pl.when(mine)(
            lambda: pltpu.make_async_copy(
                w_hbm, W7.at[yl, c, zl_src, x, yh], wr_r.at[yl]
            ).start()
        )

    def w_arrive(s):
        here = W7.at[s, cb, zl, x, yb]
        pltpu.make_async_copy(here, here, wr_r.at[s]).wait()

    def g_rows(ref, i):
        return ref.at[pl.ds(i * PATCH, PATCH)]

    def gy(i, block):
        return remote(g_rows(g_hbm, i), g_rows(G.at[block], i), gy_s.at[i], gy_r.at[i], (z, x, yh, 1 - yl, c))

    def gc(i, block):
        return remote(g_rows(g_hbm, i), g_rows(G.at[block], i), gc_s.at[i], gc_r.at[i], (z, x, yh, yl, 1 - c))

    def gf(i, block):
        part = g_rows(G.at[block], i)
        return remote(part, part, gf_s.at[i], gf_r.at[i], (z, x, yh, yl, 1 - c))

    near = (1 - yl) * 2 + c
    core = yl * 2 + 1 - c
    far = (1 - yl) * 2 + 1 - c
    for i in range(4):
        gy(i, mp).start()
    for i in range(4):
        gc(i, mp).start()

    def g_forward(i):
        gy(i, near).wait_recv()
        gf(i, near).start()

    def side(st):
        return yl if st == 0 else 1 - yl

    def block(ref, st, axis, along, across):
        zo, xo = (along, across) if axis == "z" else (across, along)
        a, b, d = bits_at[zo]
        return ref.at[side(st), d, a, x_at[xo], b]

    def half_of(ref, which):
        return ref.at[:, pl.ds(which * 384, 384)]

    def neighbour(axis, way):
        return (z_at[way], x, yh, yl, c) if axis == "z" else (z, x_at[way], yh, yl, c)

    def ag_copy(key, back):
        _, st, ph, o, way, step = key
        axis = GATHER[st][ph][0]
        ref = block(W7, st, axis, -way * back, o)
        if step == HALF[axis] - 1:
            ref = half_of(ref, 0 if way > 0 else 1)
        return remote(ref, ref, ring_s.at[ORDER[key] % POOL], ag_r.at[SLOT[key]], neighbour(axis, way))

    def rs_refs(key, off):
        _, st, ph, o, way, step = key
        axis = REDUCE[st][ph][0]
        ref, dst = block(P7, st, axis, way * off, o), landing.at[SLOT[key]]
        if step == 0:
            k = 0 if way > 0 else 1
            ref, dst = half_of(ref, k), half_of(dst, k)
        return ref, dst

    def rs_copy(key, off):
        ref, dst = rs_refs(key, off)
        to = neighbour(REDUCE[key[1]][key[2]][0], key[4])
        return remote(ref, dst, ring_s.at[ORDER[key] % POOL], rs_r.at[SLOT[key]], to)

    def send_copy(key):
        if key[0] == "ag":
            return ag_copy(key, key[5])
        return rs_copy(key, HALF[REDUCE[key[1]][key[2]][0]] - key[5])

    def receive(key):
        if key[0] == "ag":
            ag_copy(key, key[5] + 1).wait_recv()
        else:
            off = HALF[REDUCE[key[1]][key[2]][0]] - 1 - key[5]
            rs_copy(key, off).wait_recv()
            ref, got = rs_refs(key, off)
            ref[...] = (ref[...].astype(F32) + got[...].astype(F32)).astype(BF16)

    def fin_copy(st):
        s = side(st)
        return remote(P7.at[s, cb, zl, x, yb], fin.at[yh], fin_s.at[st], fin_r.at[yh], to_owner(s))

    def final(st):
        s = side(st)
        mine = is_me(to_owner(s))
        pl.when(jnp.logical_not(mine))(lambda: fin_copy(st).start())
        pl.when(mine)(
            lambda: pltpu.make_async_copy(P7.at[s, cb, zl, x, yb], fin.at[yh], fin_r.at[yh]).start()
        )

    def normed(v):
        v = v.astype(F32)
        v = v - jnp.mean(v, axis=-1, keepdims=True)
        inverse = lax.rsqrt(jnp.mean(v * v, axis=-1, keepdims=True) + EPS)
        return v * inverse, inverse

    def place(it):
        rows = pl.ds(pl.multiple_of(it // 3 * PATCH, PATCH), PATCH)
        h = rem(it, 3) * 2
        return [(rows, pl.ds(pl.multiple_of((h + n) * HD, HD), HD), pl.ds(h + n, 1), n) for n in range(2)]

    def forward(it):
        units = place(it)
        qs = [qb[rows, cols] for rows, cols, _, _ in units]
        ks = [kb[rows, cols] for rows, cols, _, _ in units]
        vs = [vb[rows, cols] for rows, cols, _, _ in units]
        a_hat = [(normed(q)[0] * qgain[u[2], :]).astype(BF16) for q, u in zip(qs, units)]
        b_hat = [(normed(k)[0] * kgain[u[2], :]).astype(BF16) for k, u in zip(ks, units)]
        scores = [dot(b, a, NT) * FACTOR for a, b in zip(a_hat, b_hat)]
        expo = [jnp.exp(s - jnp.max(s, axis=0, keepdims=True)) for s in scores]
        ps = [e * (1.0 / jnp.sum(e, axis=0, keepdims=True)) for e in expo]
        att = [dot(v, p.astype(BF16), TN).astype(BF16) for v, p in zip(vs, ps)]
        for a, b, p, t, (rows, cols, _, n) in zip(a_hat, b_hat, ps, att, units):
            qh[rows, cols] = a
            kh[rows, cols] = b
            probs[it * 2 + n] = p
            attT[cols, rows] = t

    def back(grad, normal, inverse, gain):
        u = grad * gain
        spread = jnp.mean(u * normal, axis=-1, keepdims=True)
        return ((u - jnp.mean(u, axis=-1, keepdims=True) - normal * spread) * inverse).astype(BF16)

    def backward(it):
        units = place(it)
        gas = [gatt[rows, cols] for rows, cols, _, _ in units]
        vs = [vb[rows, cols] for rows, cols, _, _ in units]
        qhs = [qh[rows, cols] for rows, cols, _, _ in units]
        khs = [kh[rows, cols] for rows, cols, _, _ in units]
        qs = [normed(qb[rows, cols]) for rows, cols, _, _ in units]
        ks = [normed(kb[rows, cols]) for rows, cols, _, _ in units]
        ps = [probs[it * 2 + n] for n in range(2)]
        gps = [dot(v, ga, NT) for v, ga in zip(vs, gas)]
        gvs = [dot(p.astype(BF16), ga, NN).astype(BF16) for p, ga in zip(ps, gas)]
        inner = [jnp.sum(p * gp, axis=0, keepdims=True) for p, gp in zip(ps, gps)]
        gss = [(p * (gp - n) * FACTOR).astype(BF16) for p, gp, n in zip(ps, gps, inner)]
        gks = [dot(g, a, NN) for g, a in zip(gss, qhs)]
        gqs = [dot(g, b, TN) for g, b in zip(gss, khs)]
        qsum = [jnp.sum(g * a, axis=0, keepdims=True) for g, (a, _) in zip(gqs, qs)]
        ksum = [jnp.sum(g * b, axis=0, keepdims=True) for g, (b, _) in zip(gks, ks)]
        qout = [back(g, a, i, qgain[u[2], :]) for g, (a, i), u in zip(gqs, qs, units)]
        kout = [back(g, b, i, kgain[u[2], :]) for g, (b, i), u in zip(gks, ks, units)]
        for (rows, cols, _, n), gv, gq, gk in zip(units, gvs, qout, kout):
            vb[rows, cols] = gv
            qb[rows, cols] = gq
            kb[rows, cols] = gk
        h = rem(it, 3) * 2
        for n in range(2):
            gacc[0, pl.ds(h + n, 1), :] += qsum[n]
            gacc[0, pl.ds(8 + h + n, 1), :] += ksum[n]

    def weight_partial(block):
        s, d = block // 2, block % 2

        def body(t, carry):
            rows = pl.ds(pl.multiple_of(t * 384, 128), 384)
            part = dot(attT[rows, :], G[block], NN).astype(BF16)
            P7[s, d, t] = part.reshape(4, 2, 48, 768)
            return carry

        lax.fori_loop(0, 2, body, 0)

    def attended_grad(t):
        rows = pl.ds(pl.multiple_of(t * 512, 512), 512)
        total = None
        for block in range(4):
            w = W7[block // 2, block % 2].reshape(768, 768)
            part = dot(G[block, rows, :], w, NT)
            total = part if total is None else total + part
        gatt[rows, :] = total.astype(BF16)

    def store(a, i):
        src, dst = ((qb, gq_hbm), (kb, gk_hbm), (vb, gv_hbm))[a]
        rows = pl.ds(i * PATCH, PATCH)
        return pltpu.make_async_copy(src.at[rows], dst.at[rows], out_sem.at[a, i])

    def gain_copy(ph, step):
        if ph == 0:
            jj = rem(j + step, 8)
            d = (z, jj // 2, jj % 2, yl, c)
        else:
            d = (rem(z + step, 8), x, yh, yl, c)
        return remote(
            gacc.at[ph], gbuf.at[ph, step - 1], ga_s.at[ph], ga_r.at[ph], d
        )

    def gain_send(ph):
        for step in range(1, 8):
            gain_copy(ph, step).start()

    def gain_out(a):
        dst = (qg_hbm, kg_hbm)[a]
        return pltpu.make_async_copy(gacc.at[2, pl.ds(a * 8, 8)], dst, small_sem.at[a])

    def gain_wait(ph, sem):
        pltpu.make_async_copy(gbuf.at[ph], gbuf.at[ph], sem.at[ph]).wait()

    def gain_sum(ph):
        gain_wait(ph, ga_r)
        total = gacc[ph]
        for step in range(1, 8):
            total = total + gbuf[ph, step - 1]
        return total

    def event(op):
        kind, what = op
        if kind == "send":
            if ORDER[what] >= POOL:
                send_copy(SENDS[ORDER[what] - POOL]).wait_send()
            send_copy(what).start()
        elif kind == "final":
            final(what)
        elif kind == "gain":
            gain_send(0)
        elif kind == "wp":
            if what == "own":
                own_load.wait()
            weight_partial({"own": mp, "core": core, "near": near, "far": far}[what])
        elif kind == "ga":
            attended_grad(what)
        elif what[0] == "wred":
            for s in range(2):
                w_arrive(s)
        elif what[0] == "gc":
            for i in range(4):
                gc(i, core).wait_recv()
        elif what[0] == "gy":
            g_forward(what[1])
        elif what[0] == "gf":
            gf(what[1], far).wait_recv()
        elif what[0] == "gain":
            total = gain_sum(what[1])
            if what[1] == 0:
                gacc[1] = total
                gain_send(1)
            else:
                gacc[2] = total
                gain_out(0).start()
                gain_out(1).start()
        else:
            receive(what)

    at = {op: n for n, op in enumerate(PLAN) if op[0] in ("fw", "bw")}
    between = {}
    for name in ("fw", "bw"):
        for i in range(12):
            end = at.get((name, i + 1), len(PLAN))
            between[name, i] = PLAN[at[name, i] + 1 : end] if i < 11 else []

    def first_body(it, carry):
        for i in range(4):
            @pl.when(it == i * 3)
            def _():
                for a in range(3):
                    load(a, i).wait()
        forward(it)
        for i in range(11):
            if between["fw", i]:
                @pl.when(it == i)
                def _():
                    for op in between["fw", i]:
                        event(op)
        return carry

    def second_body(it, carry):
        backward(it)
        for i in range(4):
            @pl.when(it == i * 3 + 2)
            def _():
                for a in range(3):
                    store(a, i).start()
        for i in range(11):
            if between["bw", i]:
                @pl.when(it == i)
                def _():
                    for op in between["bw", i]:
                        event(op)
        return carry

    gacc[...] = jnp.zeros_like(gacc)
    for op in PLAN[: at["fw", 0]]:
        event(op)
    lax.fori_loop(0, 12, first_body, 0)
    for op in PLAN[at["fw", 11] + 1 : at["bw", 0]]:
        event(op)
    lax.fori_loop(0, 12, second_body, 0)
    for op in PLAN[at["bw", 11] + 1 :]:
        event(op)

    for half in range(2):
        pl.when(jnp.logical_not(is_me(to_plane(half))))(lambda half=half: w_copy(half).wait_send())
    for i in range(4):
        gy(i, mp).wait_send()
        gc(i, mp).wait_send()
        gf(i, near).wait_send()
    for key in SENDS[-POOL:]:
        send_copy(key).wait_send()
    for ph in range(2):
        gain_wait(ph, ga_s)
    for half in range(2):
        pltpu.make_async_copy(fin.at[half], fin.at[half], fin_r.at[half]).wait()
    for st in range(2):
        pl.when(jnp.logical_not(is_me(to_owner(side(st)))))(lambda st=st: fin_copy(st).wait_send())
    gw_out[...] = fin[0].astype(F32) + fin[1].astype(F32)
    last = pltpu.make_async_copy(gw_out, gw_hbm, small_sem.at[2])
    last.start()
    for i in range(4):
        for a in range(3):
            store(a, i).wait()
    gain_out(0).wait()
    gain_out(1).wait()
    last.wait()


def hand_on(*refs):
    ins, outs, held, load_sem, store_sem = refs[:6], refs[6:12], refs[12:18], refs[18], refs[19]
    parts = []
    for a in range(6):
        pieces = 4 if a < 3 else 1
        rows = outs[a].shape[0] // pieces
        parts += [(a, pl.ds(i * rows, rows)) for i in range(pieces)]
    loads = [
        pltpu.make_async_copy(ins[a].at[part], held[a].at[part], load_sem.at[n])
        for n, (a, part) in enumerate(parts)
    ]
    stores = [
        pltpu.make_async_copy(held[a].at[part], outs[a].at[part], store_sem.at[n])
        for n, (a, part) in enumerate(parts)
    ]
    for load in loads:
        load.start()
    for load, store in zip(loads, stores):
        load.wait()
        store.start()
    for store in stores:
        store.wait()


def per_device(query_in, key_in, value_in, grad_out, out_weight, query_gain, key_gain):
    vmem = pl.BlockSpec(memory_space=pltpu.VMEM)
    anywhere = pl.BlockSpec(memory_space=pl.ANY)
    tokens = jax.ShapeDtypeStruct((1024, 768), BF16)
    dma = pltpu.SemaphoreType.DMA
    act = pltpu.VMEM((1024, 768), BF16)
    big = pltpu.VMEM((2, 2, 2, 4, 2, 48, 768), BF16)
    results = pl.pallas_call(
        kernel,
        out_shape=(
            tokens, tokens, tokens,
            jax.ShapeDtypeStruct((48, 768), F32),
            jax.ShapeDtypeStruct((8, 128), F32),
            jax.ShapeDtypeStruct((8, 128), F32),
        ),
        in_specs=[anywhere] * 5 + [vmem] * 2,
        out_specs=(anywhere,) * 6,
        scratch_shapes=[
            act, act, act,
            pltpu.VMEM((4, 1024, 768), BF16),
            big, big,
            pltpu.VMEM((768, 1024), BF16),
            act, act,
            pltpu.VMEM((24, 256, 256), F32),
            act,
            pltpu.VMEM((COPIES, 48, 768), BF16),
            pltpu.VMEM((2, 48, 768), BF16),
            pltpu.VMEM((3, 16, 128), F32),
            pltpu.VMEM((2, 7, 16, 128), F32),
            pltpu.VMEM((48, 768), F32),
            dma((3,)),
            dma((3, 4)), dma, dma((3, 4)),
            dma((2,)), dma((2,)), dma((4,)), dma((4,)), dma((4,)), dma((4,)), dma((4,)), dma((4,)),
            dma((POOL,)), dma((COPIES,)), dma((COPIES,)),
            dma((2,)), dma((2,)), dma((2,)), dma((2,)),
        ],
        compiler_params=pltpu.CompilerParams(
            collective_id=0, has_side_effects=True, vmem_limit_bytes=60 * 2**20
        ),
        cost_estimate=pl.CostEstimate(flops=12 * 10**9, bytes_accessed=12 * 10**6, transcendentals=1600000),
    )(query_in, key_in, value_in, grad_out, out_weight, query_gain, key_gain)
    return pl.pallas_call(
        hand_on,
        out_shape=(
            tokens, tokens, tokens,
            jax.ShapeDtypeStruct((48, 768), F32),
            jax.ShapeDtypeStruct((6, 128), F32),
            jax.ShapeDtypeStruct((6, 128), F32),
        ),
        in_specs=[anywhere] * 6,
        out_specs=(anywhere,) * 6,
        scratch_shapes=[
            act, act, act,
            pltpu.VMEM((48, 768), F32), pltpu.VMEM((6, 128), F32), pltpu.VMEM((6, 128), F32),
            dma((15,)), dma((15,)),
        ],
    )(*results)


def solution(mesh):
    rows = P("dp", "mp")
    heads = P("mp", None)
    return jax.shard_map(
        per_device,
        mesh=mesh,
        in_specs=(rows, rows, rows, rows, rows, heads, heads),
        out_specs=(rows, rows, rows, rows, heads, heads),
        check_vma=False,
    )
```

```python
import heapq
import itertools
import math

import jax
import jax.numpy as jnp
from jax import lax
from jax.experimental import pallas as pl
from jax.experimental.pallas import tpu as pltpu
from jax.sharding import PartitionSpec as P

PATCH = 256
HD = 128
EPS = 1e-06
F32 = jnp.float32
BF16 = jnp.bfloat16
MESH = pl.DeviceIdType.MESH
NZ, NX = 8, 4
FACTOR = 1.0 / math.sqrt(HD)

NN = (((1,), (0,)), ((), ()))
NT = (((1,), (1,)), ((), ()))
TN = (((0,), (0,)), ((), ()))


SIDES = (1, -1)
X_OUT, X_IN = (0, 1, -1, 2), (2, 1, -1, 0)
Z_OUT, Z_IN = (0, 1, -1, 2, -2, 3, -3, 4), (4, 3, -3, 2, -2, 1, -1, 0)
Z_FIRST = (("z", (0,)), ("x", Z_OUT))
GATHER = ((("x", (0,)), ("z", X_OUT)), Z_FIRST, Z_FIRST)
COLUMNS = ((0, 512), (0, 768), (512, 256))
REDUCE = ((("z", X_IN), ("x", (0,))), (("x", Z_IN), ("z", (0,))))
HALF = {"z": NZ // 2, "x": NX // 2}


def keys_of(kind, table):
    for st in range(len(table)):
        for ph in range(2):
            axis, offsets = table[st][ph]
            for o in offsets:
                for way in SIDES:
                    for step in range(HALF[axis]):
                        yield (kind, st, ph, o, way, step)


SLOT = {}
for kind, table in (("ag", GATHER), ("rs", REDUCE)):
    for number, key in enumerate(keys_of(kind, table)):
        SLOT[key] = number
GATHERS = sum(1 for key in SLOT if key[0] == "ag")
REDUCES = len(SLOT) - GATHERS

HOLD = {}
FULL, LATENCY = 1.6, 1.5
COST = {"fw": 0.95, "wp": 1.6, "wa": 1.4, "gb": 1.45, "ga": 1.45, "bw": 1.1}


def make_plan():
    now = [0.0]
    free = {}
    heap = []
    ops = []
    done = set()
    finish = [0.0]
    tally = itertools.count()

    def arrive(key, at):
        heapq.heappush(heap, (at, next(tally), key))

    def send(key):
        kind, st, ph, o, way, step = key
        axis = (GATHER if kind == "ag" else REDUCE)[st][ph][0]
        halved = step == (HALF[axis] - 1 if kind == "ag" else 0)
        start = max(now[0], free.get((axis, way), 0.0))
        share = COLUMNS[st][1] / 768 if kind == "ag" else 1.0
        free[axis, way] = start + FULL * share * (0.5 if halved else 1.0)
        arrive(key, free[axis, way] + LATENCY)
        ops.append(("send", key))

    def gather_ready(st, o):
        for way in SIDES:
            send(("ag", st, 1, o, way, 0))

    feeders = {k for k in keys_of("ag", GATHER) if k[1] > 0 and k[2] == 0}

    def try_reduce():
        if not feeders <= done:
            return
        for st, needs in ((0, ("own", "core")), (1, ("near", "far"))):
            if ("start", st) not in done and all(("wp", n) in done for n in needs):
                done.add(("start", st))
                for o in REDUCE[st][0][1]:
                    arrive(("go", st, o), now[0] + HOLD.get((st, o), 0.0))

    def try_second(st, way, step):
        half = HALF[REDUCE[st][1][0]]
        o = way * (half - step)
        if abs(o) == half:
            o = half
        axis = REDUCE[st][0][0]
        last = HALF[axis] - 1
        ready = all(("rs", st, 0, o, w, last) in done for w in SIDES)
        if ready and (step == 0 or ("rs", st, 1, 0, way, step - 1) in done):
            key = ("rs", st, 1, 0, way, step)
            if ("sent", key) not in done:
                done.add(("sent", key))
                send(key)

    def process(key):
        if key[0] == "go":
            for way in SIDES:
                send(("rs", key[1], 0, key[2], way, 0))
            return
        ops.append(("recv", key))
        done.add(key)
        now[0] += 0.05
        if key == ("wred",):
            for st in (1, 2, 0):
                for way in SIDES:
                    send(("ag", st, 0, 0, way, 0))
                gather_ready(st, 0)
        elif key[0] == "gy":
            arrive(("gf", key[1]), now[0] + 2.5)
        elif key == ("gain", 0):
            arrive(("gain", 1), now[0] + 6.0)
        elif key[0] == "ag":
            _, st, ph, o, way, step = key
            half = HALF[GATHER[st][ph][0]]
            if step + 1 < half:
                send(("ag", st, ph, o, way, step + 1))
            if ph == 0:
                if step + 1 < half:
                    gather_ready(st, -way * (step + 1))
                elif ("ag", st, 0, 0, -way, step) in done:
                    gather_ready(st, half)
            try_reduce()
        elif key[0] == "rs":
            _, st, ph, o, way, step = key
            half = HALF[REDUCE[st][ph][0]]
            if ph == 0:
                if step + 1 < half:
                    send(("rs", st, 0, o, way, step + 1))
                else:
                    for w in SIDES:
                        for later in range(HALF[REDUCE[st][1][0]]):
                            try_second(st, w, later)
            else:
                if step + 1 < half:
                    try_second(st, way, step + 1)
            total = [k for k in keys_of("rs", REDUCE) if k[1] == st]
            if all(k in done for k in total):
                ops.append(("final", st))
                finish[0] = max(finish[0], now[0] + 4.0)

    work = [("fw", i) for i in range(12)]
    work += [("wp", "own"), ("wp", "core"), ("wa", "near"), ("wa", "far"), ("wp", "near"), ("wp", "far")]
    for t in range(2):
        work += [("gb", t), ("ga", t)] + [("bw", 6 * t + i) for i in range(6)]
    gathered = [{k for k in keys_of("ag", GATHER) if k[1] == st} for st in range(3)]

    def ready(unit):
        kind, n = unit
        if kind in ("wp", "wa"):
            needs = {
                ("wp", "own"): [], ("wp", "core"): [("gc",)],
                ("wa", "near"): [("gy", 2)], ("wa", "far"): [("gf", 2)],
                ("wp", "near"): [("gy", 3), ("wa", "near")], ("wp", "far"): [("gf", 3), ("wa", "far")],
            }[unit]
            return ("fw", 11) in done and all(need in done for need in needs)
        if kind == "gb":
            return gathered[1] <= done and ("gf", 2 * n + 1) in done
        if kind == "ga":
            return gathered[0] | gathered[2] <= done and ("gb", n) in done and ("gc",) in done and ("wp", "own") in done
        if kind == "bw":
            return ("ga", n // 6) in done and (n == 0 or ("bw", n - 1) in done)
        return True

    arrive(("wred",), 6.3)
    arrive(("gc",), 8.0)
    for i in range(4):
        arrive(("gy", i), 8.4 * (i + 1) + 3.5)
    while heap or work:
        if heap and heap[0][0] <= now[0]:
            process(heapq.heappop(heap)[2])
        elif any(ready(unit) for unit in work):
            unit = next(unit for unit in work if ready(unit))
            work.remove(unit)
            ops.append(unit)
            done.add(unit)
            now[0] += COST[unit[0]]
            try_reduce()
            if unit == ("bw", 11):
                ops.append(("gain", 0))
                arrive(("gain", 0), now[0] + 3.5)
        else:
            now[0] = max(now[0], heap[0][0])
    return ops, max(now[0], finish[0])


PLAN = make_plan()[0]
POOL = 48
SENDS = [op[1] for op in PLAN if op[0] == "send"]
ORDER = {key: n for n, key in enumerate(SENDS)}


def dot(a, b, dims):
    return lax.dot_general(a, b, dims, preferred_element_type=F32)


def device(z, x, yh, yl, c):
    return {"dp": (z * NX + x) * 2 + yh, "mp": yl * 2 + c}


def kernel(
    q_hbm, k_hbm, v_hbm, g_hbm, w_hbm, qgain, kgain,
    gq_hbm, gk_hbm, gv_hbm, gw_hbm, qg_hbm, kg_hbm,
    qb, kb, vb, G, W7, P7, attT, qh, kh, probs, gatt,
    landing, fin, gacc, gbuf, gw_out, wacc, ggacc, qn, kn, inv, small_sem,
    ld_sem, own_sem, out_sem,
    wr_s, wr_r, gy_s, gy_r, gc_s, gc_r, gf_s, gf_r,
    ring_s, ag_r, rs_r, fin_s, fin_r, ga_s, ga_r,
):
    dp, mp = lax.axis_index("dp"), lax.axis_index("mp")
    z, x, yh = dp // 8, (dp // 2) % 4, dp % 2
    yl, c = mp // 2, mp % 2
    m_src, zl_src = z // 2, z % 2
    rem = lax.rem

    def bits(zz):
        r = rem(zz - 2 * mp + NZ, NZ)
        upper = (r >= 1) & (r <= 4)
        t = jnp.where(upper, r - 1, rem(NZ - r, NZ))
        return upper.astype(jnp.int32), t // 2, t % 2

    z_at = {o: rem(z + o + NZ, NZ) for o in range(-4, 5)}
    x_at = {o: rem(x + o + NX, NX) for o in range(-2, 3)}
    bits_at = {o: bits(z_at[o]) for o in range(-3, 5)}
    bits_at[-4] = bits_at[4]
    zl, yb, cb = bits_at[0]

    def to_plane(half):
        target = rem(z + (2 * zl_src - 1) * (yh * 2 + c) + NZ, NZ)
        return target, x, half, m_src // 2, m_src % 2

    def to_owner(s):
        return mp * 2 + zl, x, yb, s, cb

    def is_me(d):
        same = (d[0] == z) & (d[1] == x) & (d[2] == yh)
        return same & (d[3] == yl) & (d[4] == c)

    barrier = pltpu.get_barrier_semaphore()

    def greet(d):
        pl.semaphore_signal(barrier, inc=1, device_id=device(*d), device_id_type=MESH)

    j = x * 2 + yh
    for step in range(1, 8):
        greet((rem(z + step, 8), x, yh, yl, c))
        jj = rem(j + step, 8)
        greet((z, jj // 2, jj % 2, yl, c))
    greet((z, x, yh, 1 - yl, c))
    greet((z, x, yh, yl, 1 - c))
    count = jnp.int32(20)
    for d in (to_plane(0), to_plane(1), to_owner(0), to_owner(1)):
        mine = is_me(d)
        count = count - mine.astype(jnp.int32)
        pl.when(jnp.logical_not(mine))(lambda d=d: greet(d))

    def load(a, i):
        src, dst = ((q_hbm, qb), (k_hbm, kb), (v_hbm, vb))[a]
        rows = pl.ds(i * PATCH, PATCH)
        return pltpu.make_async_copy(src.at[rows], dst.at[rows], ld_sem.at[a, i])

    for i in range(4):
        for a in range(3):
            load(a, i).start()
    own_load = pltpu.make_async_copy(g_hbm, G.at[mp], own_sem)
    own_load.start()
    pl.semaphore_wait(barrier, count)

    def remote(src, dst, send, recv, d):
        return pltpu.make_async_remote_copy(
            src_ref=src, dst_ref=dst, send_sem=send, recv_sem=recv,
            device_id=device(*d), device_id_type=MESH,
        )

    def w_copy(half):
        return remote(w_hbm, W7.at[yl, c, zl_src, x, yh], wr_s.at[half], wr_r.at[yl], to_plane(half))

    for half in range(2):
        mine = is_me(to_plane(half))
        pl.when(jnp.logical_not(mine))(lambda half=half: w_copy(half).start())
        pl.when(mine)(
            lambda: pltpu.make_async_copy(
                w_hbm, W7.at[yl, c, zl_src, x, yh], wr_r.at[yl]
            ).start()
        )

    def w_arrive(s):
        here = W7.at[s, cb, zl, x, yb]
        pltpu.make_async_copy(here, here, wr_r.at[s]).wait()

    def g_rows(ref, i):
        return ref.at[pl.ds(i * PATCH, PATCH)]

    def gy(i, block):
        return remote(g_rows(g_hbm, i), g_rows(G.at[block], i), gy_s.at[i], gy_r.at[i], (z, x, yh, 1 - yl, c))

    def gc(i, block):
        return remote(g_rows(g_hbm, i), g_rows(G.at[block], i), gc_s.at[i], gc_r.at[i], (z, x, yh, yl, 1 - c))

    def gf(i, block):
        part = g_rows(G.at[block], i)
        return remote(part, part, gf_s.at[i], gf_r.at[i], (z, x, yh, yl, 1 - c))

    near = (1 - yl) * 2 + c
    core = yl * 2 + 1 - c
    far = (1 - yl) * 2 + 1 - c
    for i in range(4):
        gy(i, mp).start()
    for i in range(4):
        gc(i, mp).start()

    def g_forward(i):
        gy(i, near).wait_recv()
        gf(i, near).start()

    def side(st):
        return 1 - yl if st == 1 else yl

    def block(ref, st, axis, along, across):
        zo, xo = (along, across) if axis == "z" else (across, along)
        a, b, d = bits_at[zo]
        return ref.at[side(st), d, a, x_at[xo], b]

    def half_of(ref, which):
        return ref.at[:, pl.ds(which * 384, 384)]

    def neighbour(axis, way):
        return (z_at[way], x, yh, yl, c) if axis == "z" else (z, x_at[way], yh, yl, c)

    def ag_copy(key, back):
        _, st, ph, o, way, step = key
        axis = GATHER[st][ph][0]
        first, width = COLUMNS[st]
        if step == HALF[axis] - 1:
            cut = width // 2
            first, width = (first, cut) if way > 0 else (first + cut, width - cut)
        ref = block(W7, st, axis, -way * back, o).at[:, pl.ds(first, width)]
        return remote(ref, ref, ring_s.at[ORDER[key] % POOL], ag_r.at[SLOT[key]], neighbour(axis, way))

    def rs_refs(key, off):
        _, st, ph, o, way, step = key
        axis = REDUCE[st][ph][0]
        ref, dst = block(P7, st, axis, way * off, o), landing.at[SLOT[key]]
        if step == 0:
            k = 0 if way > 0 else 1
            ref, dst = half_of(ref, k), half_of(dst, k)
        return ref, dst

    def rs_copy(key, off):
        ref, dst = rs_refs(key, off)
        to = neighbour(REDUCE[key[1]][key[2]][0], key[4])
        return remote(ref, dst, ring_s.at[ORDER[key] % POOL], rs_r.at[SLOT[key]], to)

    def send_copy(key):
        if key[0] == "ag":
            return ag_copy(key, key[5])
        return rs_copy(key, HALF[REDUCE[key[1]][key[2]][0]] - key[5])

    def receive(key):
        if key[0] == "ag":
            ag_copy(key, key[5] + 1).wait_recv()
        else:
            off = HALF[REDUCE[key[1]][key[2]][0]] - 1 - key[5]
            rs_copy(key, off).wait_recv()
            ref, got = rs_refs(key, off)
            ref[...] = ref[...] + got[...]

    def fin_copy(st):
        s = side(st)
        return remote(P7.at[s, cb, zl, x, yb], fin.at[yh], fin_s.at[st], fin_r.at[yh], to_owner(s))

    def final(st):
        s = side(st)
        mine = is_me(to_owner(s))
        pl.when(jnp.logical_not(mine))(lambda: fin_copy(st).start())
        pl.when(mine)(
            lambda: pltpu.make_async_copy(P7.at[s, cb, zl, x, yb], fin.at[yh], fin_r.at[yh]).start()
        )

    def normed(v):
        v = v.astype(F32)
        v = v - jnp.mean(v, axis=-1, keepdims=True)
        inverse = lax.rsqrt(jnp.mean(v * v, axis=-1, keepdims=True) + EPS)
        return v * inverse, inverse

    def place(it):
        rows = pl.ds(pl.multiple_of(it // 3 * PATCH, PATCH), PATCH)
        h = rem(it, 3) * 2
        return [(rows, pl.ds(pl.multiple_of((h + n) * HD, HD), HD), pl.ds(h + n, 1), n) for n in range(2)]

    def forward(it):
        units = place(it)
        qs = [qb[rows, cols] for rows, cols, _, _ in units]
        ks = [kb[rows, cols] for rows, cols, _, _ in units]
        vs = [vb[rows, cols] for rows, cols, _, _ in units]
        qs = [normed(q) for q in qs]
        ks = [normed(k) for k in ks]
        a_hat = [(a * qgain[u[2], :]).astype(BF16) for (a, _), u in zip(qs, units)]
        b_hat = [(b * kgain[u[2], :]).astype(BF16) for (b, _), u in zip(ks, units)]
        scores = [dot(b, a, NT) * FACTOR for a, b in zip(a_hat, b_hat)]
        expo = [jnp.exp(s - jnp.max(s, axis=0, keepdims=True)) for s in scores]
        ps = [e * (1.0 / jnp.sum(e, axis=0, keepdims=True)) for e in expo]
        att = [dot(v, p.astype(BF16), TN).astype(BF16) for v, p in zip(vs, ps)]
        for a, b, p, t, (rows, cols, _, n) in zip(a_hat, b_hat, ps, att, units):
            qh[rows, cols] = a
            kh[rows, cols] = b
            probs[it * 2 + n] = p
            attT[cols, rows] = t
            qn[rows, cols], kn[rows, cols] = qs[n][0], ks[n][0]
            inv[it * 2 + n, :, 0:1], inv[it * 2 + n, :, 1:2] = qs[n][1], ks[n][1]

    def back(grad, normal, inverse, gain):
        u = grad * gain
        spread = jnp.mean(u * normal, axis=-1, keepdims=True)
        return ((u - jnp.mean(u, axis=-1, keepdims=True) - normal * spread) * inverse).astype(BF16)

    def backward(it):
        units = place(it)
        gas = [gatt[rows, cols] for rows, cols, _, _ in units]
        vs = [vb[rows, cols] for rows, cols, _, _ in units]
        qhs = [qh[rows, cols] for rows, cols, _, _ in units]
        khs = [kh[rows, cols] for rows, cols, _, _ in units]
        qs = [(qn[rows, cols], inv[it * 2 + n, :, 0:1]) for rows, cols, _, n in units]
        ks = [(kn[rows, cols], inv[it * 2 + n, :, 1:2]) for rows, cols, _, n in units]
        ps = [probs[it * 2 + n] for n in range(2)]
        gps = [dot(v, ga, NT) for v, ga in zip(vs, gas)]
        gvs = [dot(p.astype(BF16), ga, NN).astype(BF16) for p, ga in zip(ps, gas)]
        inner = [jnp.sum(p * gp, axis=0, keepdims=True) for p, gp in zip(ps, gps)]
        gss = [(p * (gp - n) * FACTOR).astype(BF16) for p, gp, n in zip(ps, gps, inner)]
        gks = [dot(g, a, NN) for g, a in zip(gss, qhs)]
        gqs = [dot(g, b, TN) for g, b in zip(gss, khs)]
        qsum = [jnp.sum(g * a, axis=0, keepdims=True) for g, (a, _) in zip(gqs, qs)]
        ksum = [jnp.sum(g * b, axis=0, keepdims=True) for g, (b, _) in zip(gks, ks)]
        qout = [back(g, a, i, qgain[u[2], :]) for g, (a, i), u in zip(gqs, qs, units)]
        kout = [back(g, b, i, kgain[u[2], :]) for g, (b, i), u in zip(gks, ks, units)]
        for (rows, cols, _, n), gv, gq, gk in zip(units, gvs, qout, kout):
            vb[rows, cols] = gv
            qb[rows, cols] = gq
            kb[rows, cols] = gk
        h = rem(it, 3) * 2
        for n in range(2):
            gacc[0, pl.ds(h + n, 1), :] += qsum[n]
            gacc[0, pl.ds(8 + h + n, 1), :] += ksum[n]

    def weight_partial(block):
        def body(t, carry):
            rows = pl.ds(pl.multiple_of(t * 384, 128), 384)
            part = dot(attT[rows, :], G[block], NN).astype(BF16)
            P7[block // 2, block % 2, t] = part.reshape(4, 2, 48, 768)
            return carry

        lax.fori_loop(0, 2, body, 0)

    def weight_begin(n, block):
        def body(t, carry):
            rows = pl.ds(pl.multiple_of(t * 384, 128), 384)
            wacc[n, rows, :] = dot(attT[rows, 0:768], G[block, 0:768, :], NN)
            return carry

        lax.fori_loop(0, 2, body, 0)

    def weight_end(n, block):
        def body(t, carry):
            rows = pl.ds(pl.multiple_of(t * 384, 128), 384)
            part = wacc[n, rows, :] + dot(attT[rows, 768:1024], G[block, 768:1024, :], NN)
            P7[block // 2, block % 2, t] = part.astype(BF16).reshape(4, 2, 48, 768)
            return carry

        lax.fori_loop(0, 2, body, 0)

    def attended_part(t, s):
        rows = pl.ds(pl.multiple_of(t * 512, 512), 512)
        parts = [dot(G[s * 2 + n, rows, :], W7[s, n].reshape(768, 768), NT) for n in range(2)]
        return rows, parts[0] + parts[1]

    def attended_begin(t):
        rows, part = attended_part(t, 1 - yl)
        ggacc[rows, :] = part

    def attended_end(t):
        rows, part = attended_part(t, yl)
        gatt[rows, :] = (ggacc[rows, :] + part).astype(BF16)

    def store(a, i):
        src, dst = ((qb, gq_hbm), (kb, gk_hbm), (vb, gv_hbm))[a]
        rows = pl.ds(i * PATCH, PATCH)
        return pltpu.make_async_copy(src.at[rows], dst.at[rows], out_sem.at[a, i])

    def gain_copy(ph, step):
        if ph == 0:
            jj = rem(j + step, 8)
            d = (z, jj // 2, jj % 2, yl, c)
        else:
            d = (rem(z + step, 8), x, yh, yl, c)
        return remote(
            gacc.at[ph], gbuf.at[ph, step - 1], ga_s.at[ph], ga_r.at[ph], d
        )

    def gain_send(ph):
        for step in range(1, 8):
            gain_copy(ph, step).start()

    def gain_out(a):
        dst = (qg_hbm, kg_hbm)[a]
        return pltpu.make_async_copy(gacc.at[2, pl.ds(a * 8, 8)], dst, small_sem.at[a])

    def gain_wait(ph, sem):
        pltpu.make_async_copy(gbuf.at[ph], gbuf.at[ph], sem.at[ph]).wait()

    def gain_sum(ph):
        gain_wait(ph, ga_r)
        total = gacc[ph]
        for step in range(1, 8):
            total = total + gbuf[ph, step - 1]
        return total

    def event(op):
        kind, what = op
        if kind == "send":
            if ORDER[what] >= POOL:
                send_copy(SENDS[ORDER[what] - POOL]).wait_send()
            send_copy(what).start()
        elif kind == "final":
            final(what)
        elif kind == "gain":
            gain_send(0)
        elif kind == "wp":
            if what == "own":
                own_load.wait()
            if what in ("own", "core"):
                weight_partial(mp if what == "own" else core)
            else:
                weight_end(*((0, near) if what == "near" else (1, far)))
        elif kind == "wa":
            weight_begin(*((0, near) if what == "near" else (1, far)))
        elif kind == "gb":
            attended_begin(what)
        elif kind == "ga":
            attended_end(what)
        elif what[0] == "wred":
            for s in range(2):
                w_arrive(s)
        elif what[0] == "gc":
            for i in range(4):
                gc(i, core).wait_recv()
        elif what[0] == "gy":
            g_forward(what[1])
        elif what[0] == "gf":
            gf(what[1], far).wait_recv()
        elif what[0] == "gain":
            total = gain_sum(what[1])
            if what[1] == 0:
                gacc[1] = total
                gain_send(1)
            else:
                gacc[2] = total
                gain_out(0).start()
                gain_out(1).start()
        else:
            receive(what)

    at = {op: n for n, op in enumerate(PLAN) if op[0] in ("fw", "bw")}
    between = {}
    for name in ("fw", "bw"):
        for i in range(12):
            end = at.get((name, i + 1), len(PLAN))
            between[name, i] = PLAN[at[name, i] + 1 : end] if i < 11 else []

    def first_body(it, carry):
        for i in range(4):
            @pl.when(it == i * 3)
            def _():
                for a in range(3):
                    load(a, i).wait()
        forward(it)
        for i in range(11):
            if between["fw", i]:
                @pl.when(it == i)
                def _():
                    for op in between["fw", i]:
                        event(op)
        return carry

    def second_body(it, carry):
        backward(it)
        for i in range(4):
            @pl.when(it == i * 3 + 2)
            def _():
                for a in range(3):
                    store(a, i).start()
        for i in range(11):
            if between["bw", i]:
                @pl.when(it == i)
                def _():
                    for op in between["bw", i]:
                        event(op)
        return carry

    gacc[...] = jnp.zeros_like(gacc)
    for op in PLAN[: at["fw", 0]]:
        event(op)
    lax.fori_loop(0, 12, first_body, 0)
    for op in PLAN[at["fw", 11] + 1 : at["bw", 0]]:
        event(op)
    lax.fori_loop(0, 12, second_body, 0)
    for op in PLAN[at["bw", 11] + 1 :]:
        event(op)

    for half in range(2):
        pl.when(jnp.logical_not(is_me(to_plane(half))))(lambda half=half: w_copy(half).wait_send())
    for i in range(4):
        gy(i, mp).wait_send()
        gc(i, mp).wait_send()
        gf(i, near).wait_send()
    for key in SENDS[-POOL:]:
        send_copy(key).wait_send()
    for ph in range(2):
        gain_wait(ph, ga_s)
    for half in range(2):
        pltpu.make_async_copy(fin.at[half], fin.at[half], fin_r.at[half]).wait()
    for st in range(2):
        pl.when(jnp.logical_not(is_me(to_owner(side(st)))))(lambda st=st: fin_copy(st).wait_send())
    gw_out[...] = fin[0].astype(F32) + fin[1].astype(F32)
    last = pltpu.make_async_copy(gw_out, gw_hbm, small_sem.at[2])
    last.start()
    for i in range(4):
        for a in range(3):
            store(a, i).wait()
    gain_out(0).wait()
    gain_out(1).wait()
    last.wait()


def hand_on(*refs):
    ins, outs, held, load_sem, store_sem = refs[:6], refs[6:12], refs[12:18], refs[18], refs[19]
    parts = []
    for a in range(6):
        pieces = 2 if a < 3 else 1
        rows = outs[a].shape[0] // pieces
        parts += [(a, pl.ds(i * rows, rows)) for i in range(pieces)]
    loads = [
        pltpu.make_async_copy(ins[a].at[part], held[a].at[part], load_sem.at[n])
        for n, (a, part) in enumerate(parts)
    ]
    stores = [
        pltpu.make_async_copy(held[a].at[part], outs[a].at[part], store_sem.at[n])
        for n, (a, part) in enumerate(parts)
    ]
    for load in loads:
        load.start()
    for load, store in zip(loads, stores):
        load.wait()
        store.start()
    for store in stores:
        store.wait()


def per_device(query_in, key_in, value_in, grad_out, out_weight, query_gain, key_gain):
    vmem = pl.BlockSpec(memory_space=pltpu.VMEM)
    anywhere = pl.BlockSpec(memory_space=pl.ANY)
    tokens = jax.ShapeDtypeStruct((1024, 768), BF16)
    dma = pltpu.SemaphoreType.DMA
    act = pltpu.VMEM((1024, 768), BF16)
    big = pltpu.VMEM((2, 2, 2, 4, 2, 48, 768), BF16)
    results = pl.pallas_call(
        kernel,
        out_shape=(
            tokens, tokens, tokens,
            jax.ShapeDtypeStruct((48, 768), F32),
            jax.ShapeDtypeStruct((8, 128), F32),
            jax.ShapeDtypeStruct((8, 128), F32),
        ),
        in_specs=[anywhere] * 5 + [vmem] * 2,
        out_specs=(anywhere,) * 6,
        scratch_shapes=[
            act, act, act,
            pltpu.VMEM((4, 1024, 768), BF16),
            big, big,
            pltpu.VMEM((768, 1024), BF16),
            act, act,
            pltpu.VMEM((24, 256, 256), F32),
            act,
            pltpu.VMEM((REDUCES, 48, 768), BF16),
            pltpu.VMEM((2, 48, 768), BF16),
            pltpu.VMEM((3, 16, 128), F32),
            pltpu.VMEM((2, 7, 16, 128), F32),
            pltpu.VMEM((48, 768), F32),
            pltpu.VMEM((2, 768, 768), F32),
            pltpu.VMEM((1024, 768), F32),
            pltpu.VMEM((1024, 768), F32), pltpu.VMEM((1024, 768), F32),
            pltpu.VMEM((24, 256, 2), F32),
            dma((3,)),
            dma((3, 4)), dma, dma((3, 4)),
            dma((2,)), dma((2,)), dma((4,)), dma((4,)), dma((4,)), dma((4,)), dma((4,)), dma((4,)),
            dma((POOL,)), dma((GATHERS,)), dma((REDUCES,)),
            dma((2,)), dma((2,)), dma((2,)), dma((2,)),
        ],
        compiler_params=pltpu.CompilerParams(
            collective_id=0, has_side_effects=True, vmem_limit_bytes=60 * 2**20
        ),
        cost_estimate=pl.CostEstimate(flops=12 * 10**9, bytes_accessed=12 * 10**6, transcendentals=1600000),
    )(query_in, key_in, value_in, grad_out, out_weight, query_gain, key_gain)
    return pl.pallas_call(
        hand_on,
        out_shape=(
            tokens, tokens, tokens,
            jax.ShapeDtypeStruct((48, 768), F32),
            jax.ShapeDtypeStruct((6, 128), F32),
            jax.ShapeDtypeStruct((6, 128), F32),
        ),
        in_specs=[anywhere] * 6,
        out_specs=(anywhere,) * 6,
        scratch_shapes=[
            act, act, act,
            pltpu.VMEM((48, 768), F32), pltpu.VMEM((6, 128), F32), pltpu.VMEM((6, 128), F32),
            dma((15,)), dma((15,)),
        ],
    )(*results)


def solution(mesh):
    rows = P("dp", "mp")
    heads = P("mp", None)
    return jax.shard_map(
        per_device,
        mesh=mesh,
        in_specs=(rows, rows, rows, rows, rows, heads, heads),
        out_specs=(rows, rows, rows, rows, heads, heads),
        check_vma=False,
    )
```
